32 devices in a mesh: grp: 2 (over y), patch: 4 (over z), sub: 2 (over x), pair: 2 (over core).
Axes of the slice: x: 2, y: 2, z: 4, core: 2. Of those that a mesh axis runs over, the one named last changes fastest.
Arguments:
- positions: float32 [1024, 3, 768], P(('grp', 'patch')), parts along dimension 0, may hold values from -6 to 6
- drive: float32 [1024, 3, 768], P(('grp', 'patch')), parts along dimension 0, may hold values from -6 to 6
- history: float32 [1024, 3, 768], P(('grp', 'patch', 'sub'), None, 'pair'), parts along dimension 0, may hold values from -6 to 6
- hist_dest: int32 [1024], P(('grp', 'patch', 'sub')), parts along dimension 0, may hold values from 0 to 511, as said below
- tile_target: int32 [384], P(('grp', 'patch', 'sub')), parts along dimension 0, may hold values from 0 to 127, as said below
- tile_source: int32 [384], P(('grp', 'patch', 'sub')), parts along dimension 0, may hold values from 0 to 383
- tile_count: int32 [16], P(('grp', 'patch', 'sub')), parts along dimension 0, may hold values from 1 to 24, as said below
Outputs:
- velocity: float32 [1024, 3, 768], P(('grp', 'patch', 'sub'), None, 'pair'), parts along dimension 0
- new_positions: float32 [1024, 3, 768], P(('grp', 'patch', 'sub'), None, 'pair'), parts along dimension 0
The draws below stay inside these ranges and needn't reach their ends.
There are 2 independent parts, one for each index of `grp`. The reference program is written for one: setup_inputs(seed, part) draws one part's arguments, and reference() takes and returns one part's arrays. A program takes and returns all parts, laid end to end along the dimension named above; each array names one. Nothing has to cross between parts.
Inputs may be any that keep to these rules, and one draw needn't show every extreme that they name: `tile_target`: target and source pairs of one patch's 2 * 24 slots are distinct. `tile_count`: in every draw some patch has 24 live slots in all its lists. `hist_dest`: A permutation of the panels in which dest % 128 equals the former panel's index % 128: a panel keeps its place in its block of 64, only the patch changes. The 64 panels of one block go to at most 16 per patch, a bound reached in every draw, and every block receives one panel for each place.
All inputs are finite; a program needn't handle non-finite values.
Results may differ from the reference program's by a relative error of at most 0.0003.
Values sent between devices are 32-bit elements; how exact they have to be, the bound alone decides.
A program may use at most 64 MiB of HBM per device.

```python
import math
import jax
import jax.numpy as jnp
from jax import lax

PTS = 96
PAN = 128
TD = 24
PL = 768
HB = 64
PANELS = 512
TILES_ALL = 192
N_PATCH = 4
N_SUB = 2


def tile_pairs(key):
    keys = jax.random.split(key, N_PATCH)

    def one_patch(patch_key):
        return jax.random.permutation(patch_key, 3 * PAN * PAN)[:N_SUB * TD]
    return jax.vmap(one_patch)(keys).reshape(-1).astype(jnp.int32)


def draw_tile_target(key, part):
    chosen = tile_pairs(key)
    return (chosen // (3 * PAN)).astype(jnp.int32)


def draw_tile_source(key, part):
    chosen = tile_pairs(key)
    return (chosen % (3 * PAN)).astype(jnp.int32)


def draw_tile_count(key, part):
    key = jax.random.fold_in(key, 5)
    pair_key, side_key, light_key = jax.random.split(key, 3)
    half_patches = N_PATCH // 2
    chosen = jax.random.permutation(pair_key, half_patches) < max(1, N_PATCH // 4)
    upper = jax.random.randint(side_key, (half_patches,), 0, 2)
    patch_ids = jnp.arange(N_PATCH, dtype=jnp.int32)
    pair_of = patch_ids % half_patches
    heavy = chosen[pair_of] & (patch_ids // half_patches == upper[pair_of])
    light = jax.random.randint(light_key, (N_PATCH, N_SUB), 1, TD // 2 + 1)
    return jnp.where(heavy[:, None], TD, light).reshape(-1).astype(jnp.int32)


def draw_hist_dest(key, part):
    key = jax.random.fold_in(key, 7)
    first_key, second_key = jax.random.split(key)

    def shuffle(shuffle_key):
        return jax.random.permutation(shuffle_key, N_PATCH)
    outer = jax.vmap(shuffle)(jax.random.split(first_key, N_SUB))
    inner = jax.vmap(shuffle)(jax.random.split(second_key, N_SUB))
    patch_ids = jnp.arange(N_PATCH, dtype=jnp.int32)[:, None, None]
    sub_ids = jnp.arange(N_SUB, dtype=jnp.int32)[None, :, None]
    places = jnp.arange(HB, dtype=jnp.int32)[None, None, :]
    turned = (inner[sub_ids, patch_ids] + places) % N_PATCH
    new_patch = outer[sub_ids, turned]
    return (new_patch * PAN + sub_ids * HB + places).reshape(-1).astype(jnp.int32)


def block_scale(stream_key, shape, pieces, least, top_value):
    level = 1.0
    for dim, parts in pieces:
        steps = jax.random.uniform(jax.random.fold_in(jax.random.fold_in(stream_key, 6), dim), (parts,), jnp.float32, least / len(pieces), top_value / len(pieces))
        level = level * jnp.repeat(jnp.exp(steps), shape[dim] // parts).reshape((-1,) + (1,) * (len(shape) - 1 - dim))
    return level


def scatter_about(stream_key, shape, width, bound, cuts=(), kind=jnp.bfloat16):
    gain = block_scale(stream_key, shape, cuts, -0.22, 0.18) if cuts else 1.0
    result = jax.random.normal(stream_key, shape, jnp.float32) * width * gain
    return jnp.minimum(jnp.maximum(result, -bound), bound).astype(kind)


def setup_inputs(seed: int = 0, part: int = 0) -> dict:
    seeds = jax.random.split(jax.random.key(seed), 8)
    part_keys = jax.random.split(jax.random.fold_in(seeds[7], part), 8)
    positions = scatter_about(part_keys[0], (PANELS, 3, PL), 1.0, 6.0, ((0, 4),), jnp.float32)
    drive = scatter_about(part_keys[1], (PANELS, 3, PL), 1.0, 6.0, ((0, 4),), jnp.float32)
    history = scatter_about(part_keys[2], (PANELS, 3, PL), 1.0, 6.0, ((0, 8), (2, 2)), jnp.float32)
    hist_dest = draw_hist_dest(jax.random.fold_in(jax.random.fold_in(seeds[7], part), 71), part)
    tile_target = draw_tile_target(jax.random.fold_in(jax.random.fold_in(seeds[7], part), 71), part)
    tile_source = draw_tile_source(jax.random.fold_in(jax.random.fold_in(seeds[7], part), 71), part)
    tile_count = draw_tile_count(jax.random.fold_in(jax.random.fold_in(seeds[7], part), 71), part)
    return dict(positions=positions, drive=drive, history=history, hist_dest=hist_dest, tile_target=tile_target, tile_source=tile_source, tile_count=tile_count)


EPSILON_SQ = 0.0625
SCALE_8PI = 1.0 / (8.0 * math.pi)
stiffness = 0.25
step_weight = 1.0 / 3.0

def rod_forces(positions, drive):
    panels_here, components, panel_len = positions.shape
    shaped = positions.reshape(panels_here, components, panel_len // PTS, PTS)
    before = jnp.concatenate([shaped[..., :1], shaped[..., :-1]], axis=3)
    after = jnp.concatenate([shaped[..., 1:], shaped[..., -1:]], axis=3)
    return stiffness * (before + after - 2.0 * shaped).reshape(panels_here, components, panel_len) + drive

def stokeslet(target, source, forcing):
    offset = target[:, :, None] - source[:, None, :]
    squared = lax.optimization_barrier(jnp.sum(offset * offset, axis=0))
    inverse = lax.rsqrt(squared + EPSILON_SQ)
    cube_term = inverse * inverse * inverse * SCALE_8PI
    radial = lax.optimization_barrier(jnp.sum(offset * forcing[:, None, :], axis=0)) * cube_term
    direct = lax.dot_general(forcing, (squared + 2.0 * EPSILON_SQ) * cube_term, (((1,), (1,)), ((), ())), precision=lax.Precision.HIGHEST, preferred_element_type=jnp.float32)
    return direct + lax.optimization_barrier(jnp.sum(offset * radial[None], axis=2))

def reference(positions, drive, history, hist_dest, tile_target, tile_source, tile_count):
    panel_len = positions.shape[2]
    forces = rod_forces(positions, drive)
    bundle = jnp.concatenate([positions, forces], axis=1).reshape(N_PATCH, PAN, 6, panel_len)
    zero_rim = jnp.zeros((1, PAN, 6, panel_len), bundle.dtype)
    padded = jnp.concatenate([zero_rim, bundle, zero_rim], axis=0)
    tile_ids = jnp.arange(TILES_ALL, dtype=jnp.int32)
    owner_patch = tile_ids // (N_SUB * TD)
    live_mask = tile_ids % TD < tile_count[tile_ids // TD]

    def one_tile(tile_index):
        patch_index = owner_patch[tile_index]
        source_panel = tile_source[tile_index]
        sources = padded[patch_index + source_panel // PAN, source_panel % PAN]
        target = padded[patch_index + 1, tile_target[tile_index], :3]
        return stokeslet(target, sources[:3], sources[3:])
    contributions = lax.map(one_tile, tile_ids)
    masked = jnp.where(live_mask[:, None, None], contributions, 0.0)
    segment = owner_patch * PAN + tile_target
    velocity = jax.ops.segment_sum(masked, segment, num_segments=PANELS)
    previous = jnp.zeros_like(history).at[hist_dest].set(history)
    new_positions = (4.0 * positions - previous) / 3.0 + step_weight * velocity
    return (velocity, new_positions)
```

```python
import functools
import math

import jax
import jax.numpy as jnp
from jax import lax
from jax.experimental import pallas as pl
from jax.experimental.pallas import tpu as pltpu
from jax.sharding import PartitionSpec as P

PTS = 96
EPSILON_SQ = 0.0625
SCALE_8PI = 1.0 / (8.0 * math.pi)
STIFFNESS = 0.25
CHUNK = 256

VMEM = pl.BlockSpec(memory_space=pltpu.VMEM)
SMEM = pl.BlockSpec(memory_space=pltpu.SMEM)


def cilium_forces(points, drive):
    width = points.shape[1]
    place = lax.broadcasted_iota(jnp.int32, points.shape, 1) % PTS
    before = jnp.where(place == 0, points, pltpu.roll(points, 1, 1))
    after = jnp.where(place == PTS - 1, points, pltpu.roll(points, width - 1, 1))
    return STIFFNESS * (before + after - 2.0 * points) + drive


def half_at(side, half):
    return pl.ds(pl.multiple_of(side * half, 128), half)


def pack_history_kernel(panels, info_ref, dest_ref, hist_ref, out_ref, taken):
    patches = out_ref.shape[0]
    me = info_ref[0]
    for o in range(patches):
        taken[o] = 0

    def one(b, carry):
        owner = dest_ref[b] // panels
        rel = lax.rem(owner - me + patches, patches)
        row = taken[rel]
        taken[rel] = row + 1
        for c in range(3):
            out_ref[rel, c, pl.ds(row, 1), :] = hist_ref[b, c : c + 1, :]
        return carry

    lax.fori_loop(0, hist_ref.shape[0], one, 0)


def pack_near_kernel(slots, info_ref, left_ref, right_ref, pos_ref, drive_ref, to_left, to_right):
    panels = pos_ref.shape[0]
    half = to_left.shape[2]
    lanes = half_at(info_ref[2], half)

    def one(i, msg_ref, out_ref, first):
        wanted = msg_ref[i] - first

        @pl.when((wanted >= 0) & (wanted < panels) & (i < msg_ref[slots]))
        def _():
            points = pos_ref[wanted, :, lanes]
            forces = cilium_forces(points, drive_ref[wanted, :, lanes])
            for c in range(3):
                out_ref[c, pl.ds(i, 1), :] = points[c : c + 1]
                out_ref[3 + c, pl.ds(i, 1), :] = forces[c : c + 1]

    def both(i, carry):
        one(i, right_ref, to_right, 0)
        one(i, left_ref, to_left, 2 * panels)
        return carry

    lax.fori_loop(0, slots, both, 0)


def split3(value):
    high = value.astype(jnp.bfloat16).astype(jnp.float32)
    rest = value - high
    middle = rest.astype(jnp.bfloat16).astype(jnp.float32)
    return high, middle, rest - middle


def tile_velocity(target, sources):
    center = jnp.mean(target, axis=1, keepdims=True)
    x = target - center
    width = x.shape[1]
    xx = jnp.sum(x * x, axis=0, keepdims=True)
    ones = jnp.ones((1, width), jnp.float32)
    none = jnp.zeros((3, width), jnp.float32)
    qh, qm, ql = split3(jnp.concatenate([-2.0 * x, ones, xx + EPSILON_SQ, none], axis=0))
    right = jnp.concatenate([qh, qm, qh, qm, ql, qh], axis=0).astype(jnp.bfloat16)
    total = None
    for points, force in sources:
        y = points - center
        length = y.shape[1]
        yy = jnp.sum(y * y, axis=0, keepdims=True)
        yf = jnp.sum(y * force, axis=0, keepdims=True)
        ones = jnp.ones((1, length), jnp.float32)
        none = jnp.zeros((3, length), jnp.float32)
        ph, pm, pw = split3(jnp.concatenate([y, yy, ones, none], axis=0))
        left = jnp.concatenate([ph, ph, pm, pm, ph, pw], axis=0).astype(jnp.bfloat16)
        pad = jnp.zeros((5, length), jnp.float32)
        weights = jnp.concatenate(
            [force, yf, force * y[0:1], yf * y[0:1], force * y[1:2], yf * y[1:2],
             force * y[2:3], yf * y[2:3], force * yy, pad],
            axis=0,
        )
        weights = jnp.concatenate(split3(weights), axis=0).astype(jnp.bfloat16)
        for start in range(0, length, CHUNK):
            stop = min(start + CHUNK, length)
            squared = lax.dot_general(
                left[:, start:stop], right, (((0,), (0,)), ((), ())),
                preferred_element_type=jnp.float32,
            )
            inverse = lax.rsqrt(squared)
            cube = inverse * inverse * inverse
            high = cube.astype(jnp.bfloat16)
            low = (cube - high.astype(jnp.float32)).astype(jnp.bfloat16)
            some = weights[:, start:stop]
            part = jnp.dot(some, high, preferred_element_type=jnp.float32) + jnp.dot(
                some, low, preferred_element_type=jnp.float32
            )
            total = part if total is None else total + part
    rows = total.shape[0] // 3
    total = total[2 * rows :] + total[rows : 2 * rows] + total[:rows]
    plain, along = total[0:3], total[3:4]
    by_y = [total[4 + 4 * c : 7 + 4 * c] for c in range(3)]
    along_y = [total[7 + 4 * c : 8 + 4 * c] for c in range(3)]
    lengths = total[16:19]
    direct = (xx + 2.0 * EPSILON_SQ) * plain + lengths
    for c in range(3):
        direct = direct - 2.0 * x[c : c + 1] * by_y[c]
    shared = jnp.sum(x * plain, axis=0, keepdims=True) - along
    outs = []
    for c in range(3):
        outs.append(
            SCALE_8PI
            * (
                direct[c : c + 1]
                + x[c : c + 1] * shared
                - jnp.sum(x * by_y[c], axis=0, keepdims=True)
                + along_y[c]
            )
        )
    return outs


def own_tiles_kernel(info_ref, source_ref, target_ref, count_ref, pos_ref, drive_ref, out_ref):
    panels = pos_ref.shape[0]
    half = out_ref.shape[2]
    lanes = half_at(info_ref[2], half)

    def one(i, carry):
        source = source_ref[i] - panels

        @pl.when((source >= 0) & (source < panels))
        def _():
            points = pos_ref[source]
            forces = cilium_forces(points, drive_ref[source])
            rows = tile_velocity(pos_ref[target_ref[i], :, lanes], [(points, forces)])
            for c in range(3):
                out_ref[c, pl.ds(i, 1), :] = rows[c]

        return carry

    lax.fori_loop(0, count_ref[0], one, 0)


def near_tiles_kernel(
    info_ref, source_ref, target_ref, count_ref, pos_ref, lefta, leftb, righta, rightb, own_ref, out_ref
):
    panels = pos_ref.shape[0]
    half = out_ref.shape[2]
    lanes = half_at(info_ref[2], half)
    out_ref[...] = own_ref[...]

    def halves(ref, i):
        rows = [ref[c, pl.ds(i, 1), :] for c in range(6)]
        return jnp.concatenate(rows[:3], axis=0), jnp.concatenate(rows[3:], axis=0)

    def one(i, carry):
        source = source_ref[i]

        def run(first, second):
            pa, fa = halves(first, i)
            pb, fb = halves(second, i)
            points = jnp.concatenate([pa, pb], axis=1)
            forces = jnp.concatenate([fa, fb], axis=1)
            rows = tile_velocity(pos_ref[target_ref[i], :, lanes], [(points, forces)])
            for c in range(3):
                out_ref[c, pl.ds(i, 1), :] = rows[c]

        @pl.when(source < panels)
        def _():
            run(lefta, leftb)

        @pl.when(source >= 2 * panels)
        def _():
            run(righta, rightb)

        return carry

    lax.fori_loop(0, count_ref[0], one, 0)


def finish_kernel(patches, subs, slots, *refs):
    info_ref = refs[0]
    lists = refs[1 : 1 + subs]
    dests = refs[1 + subs : 1 + subs + patches]
    pos_ref = refs[1 + subs + patches]
    shares = refs[2 + subs + patches : 2 + 2 * subs + patches]
    packed_ref = refs[2 + 2 * subs + patches]
    arrived = refs[3 + 2 * subs + patches : 2 + 2 * subs + 2 * patches]
    vel_ref, new_ref = refs[-2:]
    blocks, _, half = vel_ref.shape
    panels = pos_ref.shape[0]
    me, first, side = info_ref[0], info_ref[1] * blocks, info_ref[2]
    lanes = half_at(side, half)
    vel_ref[...] = jnp.zeros_like(vel_ref)
    for list_ref, share_ref in zip(lists, shares):

        def add(i, carry, list_ref=list_ref, share_ref=share_ref):
            place = list_ref[i] - first

            @pl.when((place >= 0) & (place < blocks))
            def _():
                for c in range(3):
                    vel_ref[place, c : c + 1, :] += share_ref[c, pl.ds(i, 1), :]

            return carry

        lax.fori_loop(0, list_ref[slots], add, 0)
    for shift in range(patches):

        def put(b, row, shift=shift):
            here = dests[shift][b] // panels == me

            @pl.when(here)
            def _():
                for c in range(3):
                    if shift == 0:
                        old = packed_ref[0, c, pl.ds(row, 1), :]
                    else:
                        old = arrived[shift - 1][c, pl.ds(row, 1), :]
                    new_ref[b, c : c + 1, :] = (
                        4.0 * pos_ref[first + b, c : c + 1, lanes] - old
                    ) / 3.0 + (1.0 / 3.0) * vel_ref[b, c : c + 1, :]

            return row + here.astype(jnp.int32)

        lax.fori_loop(0, blocks, put, 0)


def local(positions, drive, history, hist_dest, tile_target, tile_source, tile_count):
    panels = positions.shape[0]
    panel_len = positions.shape[2]
    patches, subs, pairs = (lax.axis_size(a) for a in ("patch", "sub", "pair"))
    half = panel_len // pairs
    slots = tile_target.shape[0]
    blocks = history.shape[0]
    per_peer = (blocks + patches - 1) // patches
    info = jnp.stack(
        [lax.axis_index("patch"), lax.axis_index("sub"), lax.axis_index("pair")]
    ).astype(jnp.int32)
    f32 = jnp.float32
    params = pltpu.CompilerParams(vmem_limit_bytes=48 * 1024 * 1024)

    def shifted(value, axis, shift):
        count = lax.axis_size(axis)
        return lax.ppermute(value, axis, [(i, (i + shift) % count) for i in range(count)])

    message = jnp.concatenate([tile_source, tile_count, hist_dest])
    heard = [message] + [shifted(message, "patch", s) for s in range(1, patches)]
    targets = jnp.concatenate([tile_target, tile_count])
    lists = [targets] + [shifted(targets, "sub", s) for s in range(1, subs)]
    dests = [m[slots + 1 :] for m in heard]

    packed = pl.pallas_call(
        functools.partial(pack_history_kernel, panels),
        out_shape=jax.ShapeDtypeStruct((patches, 3, per_peer, half), f32),
        in_specs=[SMEM, SMEM, VMEM],
        out_specs=VMEM,
        scratch_shapes=[pltpu.SMEM((patches,), jnp.int32)],
        compiler_params=params,
        name="pack_history",
    )(info, hist_dest, history)

    near = jax.ShapeDtypeStruct((6, slots, half), f32)
    to_left, to_right = pl.pallas_call(
        functools.partial(pack_near_kernel, slots),
        out_shape=(near, near),
        in_specs=[SMEM, SMEM, SMEM, VMEM, VMEM],
        out_specs=(VMEM, VMEM),
        compiler_params=params,
        name="pack_near",
    )(info, heard[1], heard[-1], positions, drive)

    up = [(i, i + 1) for i in range(patches - 1)]
    from_left = lax.ppermute(to_right, "patch", up)
    from_right = lax.ppermute(to_left, "patch", [(b, a) for a, b in up])

    arrived = [shifted(packed[s], "patch", s) for s in range(1, patches)]

    pairs_all = slots * half * panel_len
    own = pl.pallas_call(
        own_tiles_kernel,
        out_shape=jax.ShapeDtypeStruct((3, slots, half), f32),
        in_specs=[SMEM] * 4 + [VMEM] * 2,
        out_specs=VMEM,
        compiler_params=params,
        cost_estimate=pl.CostEstimate(
            flops=pairs_all * 256, bytes_accessed=4 * positions.size * 2, transcendentals=pairs_all
        ),
        name="own_tiles",
    )(info, tile_source, tile_target, tile_count, positions, drive)

    other_left = shifted(from_left, "pair", 1)
    other_right = shifted(from_right, "pair", 1)
    share = pl.pallas_call(
        near_tiles_kernel,
        out_shape=jax.ShapeDtypeStruct((3, slots, half), f32),
        in_specs=[SMEM] * 4 + [VMEM] * 6,
        out_specs=VMEM,
        compiler_params=params,
        cost_estimate=pl.CostEstimate(
            flops=pairs_all * 256, bytes_accessed=4 * positions.size * 2, transcendentals=pairs_all
        ),
        name="near_tiles",
    )(info, tile_source, tile_target, tile_count, positions,
      from_left, other_left, from_right, other_right, own)
    shares = [share] + [shifted(share, "sub", s) for s in range(1, subs)]

    out = jax.ShapeDtypeStruct((blocks, 3, half), f32)
    return pl.pallas_call(
        functools.partial(finish_kernel, patches, subs, slots),
        out_shape=(out, out),
        in_specs=[SMEM] * (1 + subs + patches) + [VMEM] * (1 + subs + patches),
        out_specs=(VMEM, VMEM),
        compiler_params=params,
        name="finish",
    )(info, *lists, *dests, positions, *shares, packed, *arrived)


def solution(mesh):
    by_list = P(("grp", "patch", "sub"))
    halves = P(("grp", "patch", "sub"), None, "pair")
    whole = P(("grp", "patch"), None, None)
    return jax.shard_map(
        local,
        mesh=mesh,
        in_specs=(whole, whole, halves, by_list, by_list, by_list, by_list),
        out_specs=(halves, halves),
        check_vma=False,
    )
```

```python
import functools
import math

import jax
import jax.numpy as jnp
from jax import lax
from jax.experimental import pallas as pl
from jax.experimental.pallas import tpu as pltpu
from jax.sharding import PartitionSpec as P

PTS = 96
EPSILON_SQ = 0.0625
SCALE_8PI = 1.0 / (8.0 * math.pi)
STIFFNESS = 0.25
CHUNK = 256
GROUP = 3

VMEM = pl.BlockSpec(memory_space=pltpu.VMEM)
SMEM = pl.BlockSpec(memory_space=pltpu.SMEM)


def cilium_forces(points, drive):
    width = points.shape[1]
    place = lax.broadcasted_iota(jnp.int32, points.shape, 1) % PTS
    before = jnp.where(place == 0, points, pltpu.roll(points, 1, 1))
    after = jnp.where(place == PTS - 1, points, pltpu.roll(points, width - 1, 1))
    return STIFFNESS * (before + after - 2.0 * points) + drive


def half_at(side, half):
    return pl.ds(pl.multiple_of(side * half, 128), half)


def rows_at(ref, index, lanes=slice(None), first=0):
    return jnp.concatenate(
        [ref[c, pl.ds(index, 1), lanes] for c in range(first, first + 3)], axis=0
    )


def pack_history_kernel(panels, info_ref, dest_ref, hist_ref, out_ref, taken):
    patches = out_ref.shape[0]
    me = info_ref[0]
    for o in range(patches):
        taken[o] = 0

    def one(b, carry):
        owner = dest_ref[b] // panels
        rel = lax.rem(owner - me + patches, patches)
        row = taken[rel]
        taken[rel] = row + 1
        for c in range(3):
            out_ref[rel, c, pl.ds(row, 1), :] = hist_ref[c, pl.ds(b, 1), :]
        return carry

    lax.fori_loop(0, hist_ref.shape[1], one, 0)


def pack_near_kernel(slots, info_ref, left_ref, right_ref, pos_ref, drive_ref, to_left, to_right):
    panels = pos_ref.shape[1]
    half = to_left.shape[2]
    lanes = half_at(info_ref[2], half)

    def one(i, msg_ref, out_ref, first):
        wanted = msg_ref[i] - first

        @pl.when((wanted >= 0) & (wanted < panels) & (i < msg_ref[slots]))
        def _():
            points = rows_at(pos_ref, wanted, lanes)
            forces = cilium_forces(points, rows_at(drive_ref, wanted, lanes))
            for c in range(3):
                out_ref[c, pl.ds(i, 1), :] = points[c : c + 1]
                out_ref[3 + c, pl.ds(i, 1), :] = forces[c : c + 1]

    def both(i, carry):
        one(i, right_ref, to_right, 0)
        one(i, left_ref, to_left, 2 * panels)
        return carry

    lax.fori_loop(0, slots, both, 0)


def split3(value):
    high = value.astype(jnp.bfloat16).astype(jnp.float32)
    rest = value - high
    middle = rest.astype(jnp.bfloat16).astype(jnp.float32)
    return high, middle, rest - middle


def tile_velocity(target, sources):
    center = jnp.mean(target, axis=1, keepdims=True)
    x = target - center
    width = x.shape[1]
    xx = jnp.sum(x * x, axis=0, keepdims=True)
    ones = jnp.ones((1, width), jnp.float32)
    none = jnp.zeros((3, width), jnp.float32)
    qh, qm, ql = split3(jnp.concatenate([-2.0 * x, ones, xx + EPSILON_SQ, none], axis=0))
    right = jnp.concatenate([qh, qm, qh, qm, ql, qh], axis=0).astype(jnp.bfloat16)
    total = small = None
    for points, force in sources:
        y = points - center
        length = y.shape[1]
        yy = jnp.sum(y * y, axis=0, keepdims=True)
        yf = jnp.sum(y * force, axis=0, keepdims=True)
        ones = jnp.ones((1, length), jnp.float32)
        none = jnp.zeros((3, length), jnp.float32)
        ph, pm, pw = split3(jnp.concatenate([y, yy, ones, none], axis=0))
        left = jnp.concatenate([ph, ph, pm, pm, ph, pw], axis=0).astype(jnp.bfloat16)
        pad = jnp.zeros((5, length), jnp.float32)
        weights = jnp.concatenate(
            [force, yf, force * y[0:1], yf * y[0:1], force * y[1:2], yf * y[1:2],
             force * y[2:3], yf * y[2:3], force * yy, pad],
            axis=0,
        )
        weights = jnp.concatenate(split3(weights), axis=0).astype(jnp.bfloat16)
        tail_rows = 2 * weights.shape[0] // 3
        for start in range(0, length, CHUNK):
            stop = min(start + CHUNK, length)
            squared = lax.dot_general(
                left[:, start:stop], right, (((0,), (0,)), ((), ())),
                preferred_element_type=jnp.float32,
            )
            inverse = lax.rsqrt(squared)
            cube = inverse * inverse * inverse
            high = cube.astype(jnp.bfloat16)
            low = (cube - high.astype(jnp.float32)).astype(jnp.bfloat16)
            some = weights[:, start:stop]
            part = jnp.dot(some, high, preferred_element_type=jnp.float32)
            tail = jnp.dot(some[:tail_rows], low, preferred_element_type=jnp.float32)
            total = part if total is None else total + part
            small = tail if small is None else small + tail
    rows = total.shape[0] // 3
    total = total[2 * rows :] + small[rows:] + total[rows : 2 * rows] + small[:rows] + total[:rows]
    plain, along = total[0:3], total[3:4]
    by_y = [total[4 + 4 * c : 7 + 4 * c] for c in range(3)]
    along_y = [total[7 + 4 * c : 8 + 4 * c] for c in range(3)]
    lengths = total[16:19]
    direct = (xx + 2.0 * EPSILON_SQ) * plain + lengths
    for c in range(3):
        direct = direct - 2.0 * x[c : c + 1] * by_y[c]
    shared = jnp.sum(x * plain, axis=0, keepdims=True) - along
    outs = []
    for c in range(3):
        outs.append(
            SCALE_8PI
            * (
                direct[c : c + 1]
                + x[c : c + 1] * shared
                - jnp.sum(x * by_y[c], axis=0, keepdims=True)
                + along_y[c]
            )
        )
    return outs


def each_slot(chosen, count, wanted, work):
    def note(i, found):
        chosen[found] = i
        return found + wanted(i).astype(jnp.int32)

    found = lax.fori_loop(0, count, note, 0)

    def group(j, carry):
        for k in range(GROUP):
            work(chosen[jnp.minimum(j * GROUP + k, found - 1)])
        return carry

    lax.fori_loop(0, (found + GROUP - 1) // GROUP, group, 0)


def own_tiles_kernel(info_ref, source_ref, target_ref, count_ref, pos_ref, drive_ref, out_ref, chosen):
    panels = pos_ref.shape[1]
    half = out_ref.shape[2]
    lanes = half_at(info_ref[2], half)

    def wanted(i):
        return source_ref[i] // panels == 1

    def work(i):
        source = source_ref[i] - panels
        points = rows_at(pos_ref, source)
        forces = cilium_forces(points, rows_at(drive_ref, source))
        rows = tile_velocity(rows_at(pos_ref, target_ref[i], lanes), [(points, forces)])
        for c in range(3):
            out_ref[c, pl.ds(i, 1), :] = rows[c]

    each_slot(chosen, count_ref[0], wanted, work)


def near_tiles_kernel(
    info_ref, source_ref, target_ref, count_ref, pos_ref, lefta, leftb, righta, rightb, own_ref,
    out_ref, chosen
):
    panels = pos_ref.shape[1]
    half = out_ref.shape[2]
    lanes = half_at(info_ref[2], half)
    out_ref[...] = own_ref[...]

    def wanted(i):
        return source_ref[i] // panels != 1

    def work(i):
        is_left = source_ref[i] < panels

        def both(first):
            return jnp.concatenate(
                [
                    jnp.where(is_left, rows_at(a, i, first=first), rows_at(b, i, first=first))
                    for a, b in ((lefta, righta), (leftb, rightb))
                ],
                axis=1,
            )

        rows = tile_velocity(rows_at(pos_ref, target_ref[i], lanes), [(both(0), both(3))])
        for c in range(3):
            out_ref[c, pl.ds(i, 1), :] = rows[c]

    each_slot(chosen, count_ref[0], wanted, work)


def base_kernel(patches, *refs):
    info_ref = refs[0]
    dests = refs[1 : 1 + patches]
    pos_ref, packed_ref = refs[1 + patches : 3 + patches]
    arrived = refs[3 + patches : 2 + 2 * patches]
    out_ref, places = refs[-2:]
    blocks, half = out_ref.shape[1:]
    panels = pos_ref.shape[1]
    me, side = info_ref[0], info_ref[2]
    first = pl.multiple_of(info_ref[1] * blocks, blocks)
    for shift in range(patches):
        old_ref = packed_ref.at[0] if shift == 0 else arrived[shift - 1]

        def note(b, found, shift=shift):
            places[found] = b
            return found + (dests[shift][b] // panels == me).astype(jnp.int32)

        found = lax.fori_loop(0, blocks, note, 0, unroll=8)

        def put(r, carry, old_ref=old_ref):
            for c in range(3):
                out_ref[c, pl.ds(places[r], 1), :] = old_ref[c, pl.ds(r, 1), :]
            return carry

        lax.fori_loop(0, found, put, 0)
    mine = pos_ref[:, pl.ds(first, blocks), half_at(side, half)]
    out_ref[...] = (4.0 * mine - out_ref[...]) / 3.0


def finish_kernel(subs, slots, *refs):
    info_ref = refs[0]
    lists = refs[1 : 1 + subs]
    shares = refs[1 + subs : 1 + 2 * subs]
    base_ref, vel_ref, new_ref = refs[1 + 2 * subs :]
    blocks = vel_ref.shape[1]
    first = info_ref[1] * blocks
    vel_ref[...] = jnp.zeros_like(vel_ref)
    for list_ref, share_ref in zip(lists, shares):

        def add(i, carry, list_ref=list_ref, share_ref=share_ref):
            place = list_ref[i] - first

            @pl.when((place >= 0) & (place < blocks))
            def _():
                for c in range(3):
                    vel_ref[c, pl.ds(place, 1), :] += share_ref[c, pl.ds(i, 1), :]

            return carry

        lax.fori_loop(0, list_ref[slots], add, 0)
    new_ref[...] = base_ref[...] + (1.0 / 3.0) * vel_ref[...]


def local(positions, drive, history, hist_dest, tile_target, tile_source, tile_count):
    panels = positions.shape[0]
    panel_len = positions.shape[2]
    patches, subs, pairs = (lax.axis_size(a) for a in ("patch", "sub", "pair"))
    half = panel_len // pairs
    slots = tile_target.shape[0]
    blocks = history.shape[0]
    per_peer = (blocks + patches - 1) // patches
    info = jnp.stack(
        [lax.axis_index("patch"), lax.axis_index("sub"), lax.axis_index("pair")]
    ).astype(jnp.int32)
    f32 = jnp.float32
    params = pltpu.CompilerParams(vmem_limit_bytes=48 * 1024 * 1024)
    positions, drive, history = (jnp.transpose(a, (1, 0, 2)) for a in (positions, drive, history))

    def shifted(value, axis, shift):
        count = lax.axis_size(axis)
        return lax.ppermute(value, axis, [(i, (i + shift) % count) for i in range(count)])

    message = jnp.concatenate([tile_source, tile_count, hist_dest])
    heard = [message] + [shifted(message, "patch", s) for s in range(1, patches)]
    targets = jnp.concatenate([tile_target, tile_count])
    lists = [targets] + [shifted(targets, "sub", s) for s in range(1, subs)]

    packed = pl.pallas_call(
        functools.partial(pack_history_kernel, panels),
        out_shape=jax.ShapeDtypeStruct((patches, 3, per_peer, half), f32),
        in_specs=[SMEM, SMEM, VMEM],
        out_specs=VMEM,
        scratch_shapes=[pltpu.SMEM((patches,), jnp.int32)],
        compiler_params=params,
        name="pack_history",
    )(info, hist_dest, history)
    packed, *heard = lax.optimization_barrier((packed, *heard))
    dests = [hist_dest] + [m[slots + 1 :] for m in heard[1:]]

    near = jax.ShapeDtypeStruct((6, slots, half), f32)
    to_left, to_right = pl.pallas_call(
        functools.partial(pack_near_kernel, slots),
        out_shape=(near, near),
        in_specs=[SMEM, SMEM, SMEM, VMEM, VMEM],
        out_specs=(VMEM, VMEM),
        compiler_params=params,
        name="pack_near",
    )(info, heard[1], heard[-1], positions, drive)

    up = [(i, i + 1) for i in range(patches - 1)]
    from_left = lax.ppermute(to_right, "patch", up)
    from_right = lax.ppermute(to_left, "patch", [(b, a) for a, b in up])

    arrived = [shifted(packed[s], "patch", s) for s in range(1, patches)]

    tiles = jax.ShapeDtypeStruct((3, slots, half), f32)
    chosen = [pltpu.SMEM((slots + 1,), jnp.int32)]
    pairs_all = slots * half * panel_len
    cost = pl.CostEstimate(
        flops=pairs_all * 256, bytes_accessed=4 * positions.size * 2, transcendentals=pairs_all
    )
    own = pl.pallas_call(
        own_tiles_kernel,
        out_shape=tiles,
        in_specs=[SMEM] * 4 + [VMEM] * 2,
        out_specs=VMEM,
        scratch_shapes=chosen,
        compiler_params=params,
        cost_estimate=cost,
        name="own_tiles",
    )(info, tile_source, tile_target, tile_count, positions, drive)

    other_left = shifted(from_left, "pair", 1)
    other_right = shifted(from_right, "pair", 1)
    share = pl.pallas_call(
        near_tiles_kernel,
        out_shape=tiles,
        in_specs=[SMEM] * 4 + [VMEM] * 6,
        out_specs=VMEM,
        scratch_shapes=chosen,
        compiler_params=params,
        cost_estimate=cost,
        name="near_tiles",
    )(info, tile_source, tile_target, tile_count, positions,
      from_left, other_left, from_right, other_right, own)
    shares = [share] + [shifted(share, "sub", s) for s in range(1, subs)]
    _, *arrived = lax.optimization_barrier((share, *arrived))

    out = jax.ShapeDtypeStruct((3, blocks, half), f32)
    base = pl.pallas_call(
        functools.partial(base_kernel, patches),
        out_shape=out,
        in_specs=[SMEM] * (1 + patches) + [VMEM] * (1 + patches),
        out_specs=VMEM,
        scratch_shapes=[pltpu.SMEM((blocks + 1,), jnp.int32)],
        compiler_params=params,
        name="base",
    )(info, *dests, positions, packed, *arrived)
    outs = pl.pallas_call(
        functools.partial(finish_kernel, subs, slots),
        out_shape=(out, out),
        in_specs=[SMEM] * (1 + subs) + [VMEM] * (1 + subs),
        out_specs=(VMEM, VMEM),
        compiler_params=params,
        name="finish",
    )(info, *lists, *shares, base)
    return tuple(jnp.transpose(a, (1, 0, 2)) for a in outs)


def solution(mesh):
    by_list = P(("grp", "patch", "sub"))
    halves = P(("grp", "patch", "sub"), None, "pair")
    whole = P(("grp", "patch"), None, None)
    return jax.shard_map(
        local,
        mesh=mesh,
        in_specs=(whole, whole, halves, by_list, by_list, by_list, by_list),
        out_specs=(halves, halves),
        check_vma=False,
    )
```

```python
import functools
import math

import jax
import jax.numpy as jnp
from jax import lax
from jax.experimental import pallas as pl
from jax.experimental.pallas import tpu as pltpu
from jax.sharding import PartitionSpec as P

PTS = 96
EPSILON_SQ = 0.0625
SCALE_8PI = 1.0 / (8.0 * math.pi)
STIFFNESS = 0.25
CHUNK = 768
GROUP = 4

VMEM = pl.BlockSpec(memory_space=pltpu.VMEM)
SMEM = pl.BlockSpec(memory_space=pltpu.SMEM)


def cilium_forces(points, drive):
    width = points.shape[1]
    place = lax.broadcasted_iota(jnp.int32, points.shape, 1) % PTS
    before = jnp.where(place == 0, points, pltpu.roll(points, 1, 1))
    after = jnp.where(place == PTS - 1, points, pltpu.roll(points, width - 1, 1))
    return STIFFNESS * (before + after - 2.0 * points) + drive


def half_at(side, half):
    return pl.ds(pl.multiple_of(side * half, 128), half)


def rows_at(ref, index, lanes=slice(None), first=0):
    return jnp.concatenate(
        [ref[c, pl.ds(index, 1), lanes] for c in range(first, first + 3)], axis=0
    )


def pack_history_kernel(panels, info_ref, dest_ref, hist_ref, out_ref, taken):
    patches = out_ref.shape[0]
    me = info_ref[0]
    for o in range(patches):
        taken[o] = 0

    def one(b, carry):
        owner = dest_ref[b] // panels
        rel = lax.rem(owner - me + patches, patches)
        row = taken[rel]
        taken[rel] = row + 1
        for c in range(3):
            out_ref[rel, c, pl.ds(row, 1), :] = hist_ref[c, pl.ds(b, 1), :]
        return carry

    lax.fori_loop(0, hist_ref.shape[1], one, 0)


def pack_near_kernel(slots, info_ref, left_ref, right_ref, pos_ref, drive_ref, to_left, to_right):
    panels = pos_ref.shape[1]
    half = to_left.shape[2]
    lanes = half_at(info_ref[2], half)

    def one(i, msg_ref, out_ref, first):
        wanted = msg_ref[i] - first

        @pl.when((wanted >= 0) & (wanted < panels) & (i < msg_ref[slots]))
        def _():
            points = rows_at(pos_ref, wanted, lanes)
            forces = cilium_forces(points, rows_at(drive_ref, wanted, lanes))
            for c in range(3):
                out_ref[c, pl.ds(i, 1), :] = points[c : c + 1]
                out_ref[3 + c, pl.ds(i, 1), :] = forces[c : c + 1]

    def both(i, carry):
        one(i, right_ref, to_right, 0)
        one(i, left_ref, to_left, 2 * panels)
        return carry

    lax.fori_loop(0, slots, both, 0)


def split3(value):
    high = value.astype(jnp.bfloat16).astype(jnp.float32)
    rest = value - high
    middle = rest.astype(jnp.bfloat16).astype(jnp.float32)
    return high, middle, rest - middle


def tile_velocity(target, sources):
    center = jnp.mean(target, axis=1, keepdims=True)
    x = target - center
    width = x.shape[1]
    xx = jnp.sum(x * x, axis=0, keepdims=True)
    ones = jnp.ones((1, width), jnp.float32)
    none = jnp.zeros((3, width), jnp.float32)
    qh, qm, ql = split3(jnp.concatenate([-2.0 * x, ones, xx + EPSILON_SQ, none], axis=0))
    right = jnp.concatenate([qh, qm, qh, qm, ql, qh], axis=0).astype(jnp.bfloat16)
    total = small = None
    for points, force in sources:
        y = points - center
        length = y.shape[1]
        yy = jnp.sum(y * y, axis=0, keepdims=True)
        yf = jnp.sum(y * force, axis=0, keepdims=True)
        ones = jnp.ones((1, length), jnp.float32)
        none = jnp.zeros((3, length), jnp.float32)
        ph, pm, pw = split3(jnp.concatenate([y, yy, ones, none], axis=0))
        left = jnp.concatenate([ph, ph, pm, pm, ph, pw], axis=0).astype(jnp.bfloat16)
        pad = jnp.zeros((5, length), jnp.float32)
        weights = jnp.concatenate(
            [force, yf, force * y[0:1], yf * y[0:1], force * y[1:2], yf * y[1:2],
             force * y[2:3], yf * y[2:3], force * yy, pad],
            axis=0,
        )
        weights = jnp.concatenate(split3(weights), axis=0).astype(jnp.bfloat16)
        tail_rows = 2 * weights.shape[0] // 3
        for start in range(0, length, CHUNK):
            stop = min(start + CHUNK, length)
            squared = lax.dot_general(
                left[:, start:stop], right, (((0,), (0,)), ((), ())),
                preferred_element_type=jnp.float32,
            )
            inverse = lax.rsqrt(squared)
            cube = inverse * inverse * inverse
            high = cube.astype(jnp.bfloat16)
            low = (cube - high.astype(jnp.float32)).astype(jnp.bfloat16)
            some = weights[:, start:stop]
            part = jnp.dot(some, high, preferred_element_type=jnp.float32)
            tail = jnp.dot(some[:tail_rows], low, preferred_element_type=jnp.float32)
            total = part if total is None else total + part
            small = tail if small is None else small + tail
    rows = total.shape[0] // 3
    total = total[2 * rows :] + small[rows:] + total[rows : 2 * rows] + small[:rows] + total[:rows]
    plain, along = total[0:3], total[3:4]
    by_y = [total[4 + 4 * c : 7 + 4 * c] for c in range(3)]
    along_y = [total[7 + 4 * c : 8 + 4 * c] for c in range(3)]
    lengths = total[16:19]
    direct = (xx + 2.0 * EPSILON_SQ) * plain + lengths
    for c in range(3):
        direct = direct - 2.0 * x[c : c + 1] * by_y[c]
    shared = jnp.sum(x * plain, axis=0, keepdims=True) - along
    outs = []
    for c in range(3):
        outs.append(
            SCALE_8PI
            * (
                direct[c : c + 1]
                + x[c : c + 1] * shared
                - jnp.sum(x * by_y[c], axis=0, keepdims=True)
                + along_y[c]
            )
        )
    return outs


def each_slot(chosen, count, wanted, work):
    def note(i, found):
        chosen[found] = i
        return found + wanted(i).astype(jnp.int32)

    found = lax.fori_loop(0, count, note, 0)

    def group(j, carry):
        for k in range(GROUP):
            work(chosen[jnp.minimum(j * GROUP + k, found - 1)])
        return carry

    lax.fori_loop(0, (found + GROUP - 1) // GROUP, group, 0)


def own_tiles_kernel(info_ref, source_ref, target_ref, count_ref, pos_ref, drive_ref, out_ref, chosen):
    panels = pos_ref.shape[1]
    half = out_ref.shape[2]
    lanes = half_at(info_ref[2], half)

    def wanted(i):
        return source_ref[i] // panels == 1

    def work(i):
        source = source_ref[i] - panels
        points = rows_at(pos_ref, source)
        forces = cilium_forces(points, rows_at(drive_ref, source))
        rows = tile_velocity(rows_at(pos_ref, target_ref[i], lanes), [(points, forces)])
        for c in range(3):
            out_ref[c, pl.ds(i, 1), :] = rows[c]

    each_slot(chosen, count_ref[0], wanted, work)


def near_tiles_kernel(
    info_ref, source_ref, target_ref, count_ref, pos_ref, lefta, leftb, righta, rightb, own_ref,
    out_ref, chosen
):
    panels = pos_ref.shape[1]
    half = out_ref.shape[2]
    lanes = half_at(info_ref[2], half)
    out_ref[...] = own_ref[...]

    def wanted(i):
        return source_ref[i] // panels != 1

    def work(i):
        is_left = source_ref[i] < panels

        def both(first):
            return jnp.concatenate(
                [
                    jnp.where(is_left, rows_at(a, i, first=first), rows_at(b, i, first=first))
                    for a, b in ((lefta, righta), (leftb, rightb))
                ],
                axis=1,
            )

        rows = tile_velocity(rows_at(pos_ref, target_ref[i], lanes), [(both(0), both(3))])
        for c in range(3):
            out_ref[c, pl.ds(i, 1), :] = rows[c]

    each_slot(chosen, count_ref[0], wanted, work)


def base_kernel(patches, *refs):
    info_ref = refs[0]
    dests = refs[1 : 1 + patches]
    pos_ref, packed_ref = refs[1 + patches : 3 + patches]
    arrived = refs[3 + patches : 2 + 2 * patches]
    out_ref, places = refs[-2:]
    blocks, half = out_ref.shape[1:]
    panels = pos_ref.shape[1]
    me, side = info_ref[0], info_ref[2]
    first = pl.multiple_of(info_ref[1] * blocks, blocks)
    for shift in range(patches):
        old_ref = packed_ref.at[0] if shift == 0 else arrived[shift - 1]

        def note(b, found, shift=shift):
            places[found] = b
            return found + (dests[shift][b] // panels == me).astype(jnp.int32)

        found = lax.fori_loop(0, blocks, note, 0, unroll=8)

        def put(r, carry, old_ref=old_ref):
            for c in range(3):
                out_ref[c, pl.ds(places[r], 1), :] = old_ref[c, pl.ds(r, 1), :]
            return carry

        lax.fori_loop(0, found, put, 0)
    mine = pos_ref[:, pl.ds(first, blocks), half_at(side, half)]
    out_ref[...] = (4.0 * mine - out_ref[...]) / 3.0


def finish_kernel(subs, slots, *refs):
    info_ref = refs[0]
    lists = refs[1 : 1 + subs]
    shares = refs[1 + subs : 1 + 2 * subs]
    base_ref, vel_ref, new_ref = refs[1 + 2 * subs :]
    blocks = vel_ref.shape[1]
    first = info_ref[1] * blocks
    vel_ref[...] = jnp.zeros_like(vel_ref)
    for list_ref, share_ref in zip(lists, shares):

        def add(i, carry, list_ref=list_ref, share_ref=share_ref):
            place = list_ref[i] - first

            @pl.when((place >= 0) & (place < blocks))
            def _():
                for c in range(3):
                    vel_ref[c, pl.ds(place, 1), :] += share_ref[c, pl.ds(i, 1), :]

            return carry

        lax.fori_loop(0, list_ref[slots], add, 0)
    new_ref[...] = base_ref[...] + (1.0 / 3.0) * vel_ref[...]


def local(positions, drive, history, hist_dest, tile_target, tile_source, tile_count):
    panels = positions.shape[0]
    panel_len = positions.shape[2]
    patches, subs, pairs = (lax.axis_size(a) for a in ("patch", "sub", "pair"))
    half = panel_len // pairs
    slots = tile_target.shape[0]
    blocks = history.shape[0]
    per_peer = (blocks + patches - 1) // patches
    info = jnp.stack(
        [lax.axis_index("patch"), lax.axis_index("sub"), lax.axis_index("pair")]
    ).astype(jnp.int32)
    f32 = jnp.float32
    params = pltpu.CompilerParams(vmem_limit_bytes=48 * 1024 * 1024)
    positions, drive, history = (jnp.transpose(a, (1, 0, 2)) for a in (positions, drive, history))

    def shifted(value, axis, shift):
        count = lax.axis_size(axis)
        return lax.ppermute(value, axis, [(i, (i + shift) % count) for i in range(count)])

    message = jnp.concatenate([tile_source, tile_count, hist_dest])
    heard = [message] + [shifted(message, "patch", s) for s in range(1, patches)]
    targets = jnp.concatenate([tile_target, tile_count])
    lists = [targets] + [shifted(targets, "sub", s) for s in range(1, subs)]

    packed = pl.pallas_call(
        functools.partial(pack_history_kernel, panels),
        out_shape=jax.ShapeDtypeStruct((patches, 3, per_peer, half), f32),
        in_specs=[SMEM, SMEM, VMEM],
        out_specs=VMEM,
        scratch_shapes=[pltpu.SMEM((patches,), jnp.int32)],
        compiler_params=params,
        name="pack_history",
    )(info, hist_dest, history)
    packed, *heard = lax.optimization_barrier((packed, *heard))
    dests = [hist_dest] + [m[slots + 1 :] for m in heard[1:]]

    near = jax.ShapeDtypeStruct((6, slots, half), f32)
    to_left, to_right = pl.pallas_call(
        functools.partial(pack_near_kernel, slots),
        out_shape=(near, near),
        in_specs=[SMEM, SMEM, SMEM, VMEM, VMEM],
        out_specs=(VMEM, VMEM),
        compiler_params=params,
        name="pack_near",
    )(info, heard[1], heard[-1], positions, drive)

    up = [(i, i + 1) for i in range(patches - 1)]
    from_left = lax.ppermute(to_right, "patch", up)
    from_right = lax.ppermute(to_left, "patch", [(b, a) for a, b in up])

    arrived = [shifted(packed[s], "patch", s) for s in range(1, patches)]

    tiles = jax.ShapeDtypeStruct((3, slots, half), f32)
    chosen = [pltpu.SMEM((slots + 1,), jnp.int32)]
    pairs_all = slots * half * panel_len
    cost = pl.CostEstimate(
        flops=pairs_all * 256, bytes_accessed=4 * positions.size * 2, transcendentals=pairs_all
    )
    own = pl.pallas_call(
        own_tiles_kernel,
        out_shape=tiles,
        in_specs=[SMEM] * 4 + [VMEM] * 2,
        out_specs=VMEM,
        scratch_shapes=chosen,
        compiler_params=params,
        cost_estimate=cost,
        name="own_tiles",
    )(info, tile_source, tile_target, tile_count, positions, drive)

    own, *lists = lax.optimization_barrier((own, *lists))
    other_left = shifted(from_left, "pair", 1)
    other_right = shifted(from_right, "pair", 1)
    share = pl.pallas_call(
        near_tiles_kernel,
        out_shape=tiles,
        in_specs=[SMEM] * 4 + [VMEM] * 6,
        out_specs=VMEM,
        scratch_shapes=chosen,
        compiler_params=params,
        cost_estimate=cost,
        name="near_tiles",
    )(info, tile_source, tile_target, tile_count, positions,
      from_left, other_left, from_right, other_right, own)
    shares = [share] + [shifted(share, "sub", s) for s in range(1, subs)]
    _, *arrived = lax.optimization_barrier((share, *arrived))

    out = jax.ShapeDtypeStruct((3, blocks, half), f32)
    base = pl.pallas_call(
        functools.partial(base_kernel, patches),
        out_shape=out,
        in_specs=[SMEM] * (1 + patches) + [VMEM] * (1 + patches),
        out_specs=VMEM,
        scratch_shapes=[pltpu.SMEM((blocks + 1,), jnp.int32)],
        compiler_params=params,
        name="base",
    )(info, *dests, positions, packed, *arrived)
    outs = pl.pallas_call(
        functools.partial(finish_kernel, subs, slots),
        out_shape=(out, out),
        in_specs=[SMEM] * (1 + subs) + [VMEM] * (1 + subs),
        out_specs=(VMEM, VMEM),
        compiler_params=params,
        name="finish",
    )(info, *lists, *shares, base)
    return tuple(jnp.transpose(a, (1, 0, 2)) for a in outs)


def solution(mesh):
    by_list = P(("grp", "patch", "sub"))
    halves = P(("grp", "patch", "sub"), None, "pair")
    whole = P(("grp", "patch"), None, None)
    return jax.shard_map(
        local,
        mesh=mesh,
        in_specs=(whole, whole, halves, by_list, by_list, by_list, by_list),
        out_specs=(halves, halves),
        check_vma=False,
    )
```

```python
import functools
import math

import jax
import jax.numpy as jnp
from jax import lax
from jax.experimental import pallas as pl
from jax.experimental.pallas import tpu as pltpu
from jax.sharding import PartitionSpec as P

PTS = 96
EPSILON_SQ = 0.0625
SCALE_8PI = 1.0 / (8.0 * math.pi)
STIFFNESS = 0.25
CHUNK = 768
GROUP = 4

VMEM = pl.BlockSpec(memory_space=pltpu.VMEM)
SMEM = pl.BlockSpec(memory_space=pltpu.SMEM)


def cilium_forces(points, drive):
    width = points.shape[1]
    place = lax.broadcasted_iota(jnp.int32, points.shape, 1) % PTS
    before = jnp.where(place == 0, points, pltpu.roll(points, 1, 1))
    after = jnp.where(place == PTS - 1, points, pltpu.roll(points, width - 1, 1))
    return STIFFNESS * (before + after - 2.0 * points) + drive


def half_at(side, half):
    return pl.ds(pl.multiple_of(side * half, 128), half)


def rows_at(ref, index, lanes=slice(None), first=0):
    return jnp.concatenate(
        [ref[c, pl.ds(index, 1), lanes] for c in range(first, first + 3)], axis=0
    )


def pack_history_kernel(panels, info_ref, dest_ref, hist_ref, out_ref, taken):
    patches = out_ref.shape[0]
    me = info_ref[0]
    for o in range(patches):
        taken[o] = 0

    def one(b, carry):
        owner = dest_ref[b] // panels
        rel = lax.rem(owner - me + patches, patches)
        row = taken[rel]
        taken[rel] = row + 1
        for c in range(3):
            out_ref[rel, c, pl.ds(row, 1), :] = hist_ref[c, pl.ds(b, 1), :]
        return carry

    lax.fori_loop(0, hist_ref.shape[1], one, 0)


def pack_near_kernel(slots, info_ref, left_ref, right_ref, pos_ref, drive_ref, to_left, to_right):
    panels = pos_ref.shape[1]
    half = to_left.shape[2]
    lanes = half_at(info_ref[2], half)

    def one(i, msg_ref, out_ref, first):
        wanted = msg_ref[i] - first

        @pl.when((wanted >= 0) & (wanted < panels) & (i < msg_ref[slots]))
        def _():
            points = rows_at(pos_ref, wanted, lanes)
            forces = cilium_forces(points, rows_at(drive_ref, wanted, lanes))
            for c in range(3):
                out_ref[c, pl.ds(i, 1), :] = points[c : c + 1]
                out_ref[3 + c, pl.ds(i, 1), :] = forces[c : c + 1]

    def both(i, carry):
        one(i, right_ref, to_right, 0)
        one(i, left_ref, to_left, 2 * panels)
        return carry

    lax.fori_loop(0, slots, both, 0)


def split3(value):
    high = value.astype(jnp.bfloat16).astype(jnp.float32)
    rest = value - high
    middle = rest.astype(jnp.bfloat16).astype(jnp.float32)
    return high, middle, rest - middle


def tile_velocity(target, sources):
    center = jnp.mean(target, axis=1, keepdims=True)
    x = target - center
    width = x.shape[1]
    xx = jnp.sum(x * x, axis=0, keepdims=True)
    ones = jnp.ones((1, width), jnp.float32)
    none = jnp.zeros((3, width), jnp.float32)
    qh, qm, ql = split3(jnp.concatenate([-2.0 * x, ones, xx + EPSILON_SQ, none], axis=0))
    right = jnp.concatenate([qh, qm, qh, qm, ql, qh], axis=0).astype(jnp.bfloat16)
    total = small = None
    for points, force in sources:
        y = points - center
        length = y.shape[1]
        yy = jnp.sum(y * y, axis=0, keepdims=True)
        yf = jnp.sum(y * force, axis=0, keepdims=True)
        ones = jnp.ones((1, length), jnp.float32)
        none = jnp.zeros((3, length), jnp.float32)
        ph, pm, pw = split3(jnp.concatenate([y, yy, ones, none], axis=0))
        left = jnp.concatenate([ph, ph, pm, pm, ph, pw], axis=0).astype(jnp.bfloat16)
        pad = jnp.zeros((5, length), jnp.float32)
        weights = jnp.concatenate(
            [force, yf, force * y[0:1], yf * y[0:1], force * y[1:2], yf * y[1:2],
             force * y[2:3], yf * y[2:3], force * yy, pad],
            axis=0,
        )
        weights = jnp.concatenate(split3(weights), axis=0).astype(jnp.bfloat16)
        tail_rows = 2 * weights.shape[0] // 3
        for start in range(0, length, CHUNK):
            stop = min(start + CHUNK, length)
            squared = lax.dot_general(
                left[:, start:stop], right, (((0,), (0,)), ((), ())),
                preferred_element_type=jnp.float32,
            )
            inverse = lax.rsqrt(squared)
            cube = inverse * inverse * inverse
            high = cube.astype(jnp.bfloat16)
            low = (cube - high.astype(jnp.float32)).astype(jnp.bfloat16)
            some = weights[:, start:stop]
            part = jnp.dot(some, high, preferred_element_type=jnp.float32)
            tail = jnp.dot(some[:tail_rows], low, preferred_element_type=jnp.float32)
            total = part if total is None else total + part
            small = tail if small is None else small + tail
    rows = total.shape[0] // 3
    total = total[2 * rows :] + small[rows:] + total[rows : 2 * rows] + small[:rows] + total[:rows]
    plain, along = total[0:3], total[3:4]
    by_y = [total[4 + 4 * c : 7 + 4 * c] for c in range(3)]
    along_y = [total[7 + 4 * c : 8 + 4 * c] for c in range(3)]
    lengths = total[16:19]
    direct = (xx + 2.0 * EPSILON_SQ) * plain + lengths
    for c in range(3):
        direct = direct - 2.0 * x[c : c + 1] * by_y[c]
    shared = jnp.sum(x * plain, axis=0, keepdims=True) - along
    outs = []
    for c in range(3):
        outs.append(
            SCALE_8PI
            * (
                direct[c : c + 1]
                + x[c : c + 1] * shared
                - jnp.sum(x * by_y[c], axis=0, keepdims=True)
                + along_y[c]
            )
        )
    return outs


def each_slot(chosen, count, wanted, work):
    def note(i, found):
        chosen[found] = i
        return found + wanted(i).astype(jnp.int32)

    found = lax.fori_loop(0, count, note, 0)

    def group(j, carry):
        for k in range(GROUP):
            work(chosen[jnp.minimum(j * GROUP + k, found - 1)])
        return carry

    lax.fori_loop(0, (found + GROUP - 1) // GROUP, group, 0)


def own_tiles_kernel(info_ref, source_ref, target_ref, count_ref, pos_ref, drive_ref, out_ref, chosen):
    panels = pos_ref.shape[1]
    half = out_ref.shape[2]
    lanes = half_at(info_ref[2], half)

    def wanted(i):
        return source_ref[i] // panels == 1

    def work(i):
        source = source_ref[i] - panels
        points = rows_at(pos_ref, source)
        forces = cilium_forces(points, rows_at(drive_ref, source))
        rows = tile_velocity(rows_at(pos_ref, target_ref[i], lanes), [(points, forces)])
        for c in range(3):
            out_ref[c, pl.ds(i, 1), :] = rows[c]

    each_slot(chosen, count_ref[0], wanted, work)


def near_tiles_kernel(
    info_ref, source_ref, target_ref, count_ref, pos_ref, lefta, leftb, righta, rightb, own_ref,
    out_ref, chosen
):
    panels = pos_ref.shape[1]
    half = out_ref.shape[2]
    lanes = half_at(info_ref[2], half)
    out_ref[...] = own_ref[...]

    def wanted(i):
        return source_ref[i] // panels != 1

    def work(i):
        is_left = source_ref[i] < panels

        def both(first):
            return jnp.concatenate(
                [
                    jnp.where(is_left, rows_at(a, i, first=first), rows_at(b, i, first=first))
                    for a, b in ((lefta, righta), (leftb, rightb))
                ],
                axis=1,
            )

        rows = tile_velocity(rows_at(pos_ref, target_ref[i], lanes), [(both(0), both(3))])
        for c in range(3):
            out_ref[c, pl.ds(i, 1), :] = rows[c]

    each_slot(chosen, count_ref[0], wanted, work)


def base_kernel(patches, *refs):
    info_ref = refs[0]
    dests = refs[1 : 1 + patches]
    pos_ref, packed_ref = refs[1 + patches : 3 + patches]
    arrived = refs[3 + patches : 2 + 2 * patches]
    out_ref, places = refs[-2:]
    blocks, half = out_ref.shape[1:]
    panels = pos_ref.shape[1]
    me, side = info_ref[0], info_ref[2]
    first = pl.multiple_of(info_ref[1] * blocks, blocks)
    for shift in range(patches):
        old_ref = packed_ref.at[0] if shift == 0 else arrived[shift - 1]

        def note(b, found, shift=shift):
            places[found] = b
            return found + (dests[shift][b] // panels == me).astype(jnp.int32)

        found = lax.fori_loop(0, blocks, note, 0, unroll=8)

        def put(r, carry, old_ref=old_ref):
            for c in range(3):
                out_ref[c, pl.ds(places[r], 1), :] = old_ref[c, pl.ds(r, 1), :]
            return carry

        lax.fori_loop(0, found, put, 0)
    mine = pos_ref[:, pl.ds(first, blocks), half_at(side, half)]
    out_ref[...] = (4.0 * mine - out_ref[...]) / 3.0


def finish_kernel(subs, slots, *refs):
    info_ref = refs[0]
    lists = refs[1 : 1 + subs]
    shares = refs[1 + subs : 1 + 2 * subs]
    base_ref, vel_ref, new_ref = refs[1 + 2 * subs :]
    blocks = vel_ref.shape[1]
    first = info_ref[1] * blocks
    vel_ref[...] = jnp.zeros_like(vel_ref)
    for list_ref, share_ref in zip(lists, shares):

        def add(i, carry, list_ref=list_ref, share_ref=share_ref):
            place = list_ref[i] - first

            @pl.when((place >= 0) & (place < blocks))
            def _():
                for c in range(3):
                    vel_ref[c, pl.ds(place, 1), :] += share_ref[c, pl.ds(i, 1), :]

            return carry

        lax.fori_loop(0, list_ref[slots], add, 0)
    new_ref[...] = base_ref[...] + (1.0 / 3.0) * vel_ref[...]


def local(positions, drive, history, hist_dest, tile_target, tile_source, tile_count):
    panels = positions.shape[0]
    panel_len = positions.shape[2]
    patches, subs, pairs = (lax.axis_size(a) for a in ("patch", "sub", "pair"))
    half = panel_len // pairs
    slots = tile_target.shape[0]
    blocks = history.shape[0]
    per_peer = (blocks + patches - 1) // patches
    info = jnp.stack(
        [lax.axis_index("patch"), lax.axis_index("sub"), lax.axis_index("pair")]
    ).astype(jnp.int32)
    f32 = jnp.float32
    params = pltpu.CompilerParams(vmem_limit_bytes=48 * 1024 * 1024)
    positions, drive, history = (jnp.transpose(a, (1, 0, 2)) for a in (positions, drive, history))

    def shifted(value, axis, shift):
        count = lax.axis_size(axis)
        return lax.ppermute(value, axis, [(i, (i + shift) % count) for i in range(count)])

    message = jnp.concatenate([tile_source, tile_count, hist_dest])
    heard = [message] + [shifted(message, "patch", s) for s in range(1, patches)]
    targets = jnp.concatenate([tile_target, tile_count])
    lists = [targets] + [shifted(targets, "sub", s) for s in range(1, subs)]

    packed = pl.pallas_call(
        functools.partial(pack_history_kernel, panels),
        out_shape=jax.ShapeDtypeStruct((patches, 3, per_peer, half), f32),
        in_specs=[SMEM, SMEM, VMEM],
        out_specs=VMEM,
        scratch_shapes=[pltpu.SMEM((patches,), jnp.int32)],
        compiler_params=params,
        name="pack_history",
    )(info, hist_dest, history)
    packed, *heard = lax.optimization_barrier((packed, *heard))
    dests = [hist_dest] + [m[slots + 1 :] for m in heard[1:]]

    near = jax.ShapeDtypeStruct((6, slots, half), f32)
    to_left, to_right = pl.pallas_call(
        functools.partial(pack_near_kernel, slots),
        out_shape=(near, near),
        in_specs=[SMEM, SMEM, SMEM, VMEM, VMEM],
        out_specs=(VMEM, VMEM),
        compiler_params=params,
        name="pack_near",
    )(info, heard[1], heard[-1], positions, drive)

    up = [(i, i + 1) for i in range(patches - 1)]
    from_left = lax.ppermute(to_right, "patch", up)
    from_right = lax.ppermute(to_left, "patch", [(b, a) for a, b in up])

    arrived = [shifted(packed[s], "patch", s) for s in range(1, patches)]

    tiles = jax.ShapeDtypeStruct((3, slots, half), f32)
    chosen = [pltpu.SMEM((slots + 1,), jnp.int32)]
    pairs_all = slots * half * panel_len
    cost = pl.CostEstimate(
        flops=pairs_all * 256, bytes_accessed=4 * positions.size * 2, transcendentals=pairs_all
    )
    own = pl.pallas_call(
        own_tiles_kernel,
        out_shape=tiles,
        in_specs=[SMEM] * 4 + [VMEM] * 2,
        out_specs=VMEM,
        scratch_shapes=chosen,
        compiler_params=params,
        cost_estimate=cost,
        name="own_tiles",
    )(info, tile_source, tile_target, tile_count, positions, drive)

    other_left = shifted(from_left, "pair", 1)
    other_right = shifted(from_right, "pair", 1)
    share = pl.pallas_call(
        near_tiles_kernel,
        out_shape=tiles,
        in_specs=[SMEM] * 4 + [VMEM] * 6,
        out_specs=VMEM,
        scratch_shapes=chosen,
        compiler_params=params,
        cost_estimate=cost,
        name="near_tiles",
    )(info, tile_source, tile_target, tile_count, positions,
      from_left, other_left, from_right, other_right, own)
    shares = [share] + [shifted(share, "sub", s) for s in range(1, subs)]
    _, *arrived = lax.optimization_barrier((share, *arrived))

    out = jax.ShapeDtypeStruct((3, blocks, half), f32)
    base = pl.pallas_call(
        functools.partial(base_kernel, patches),
        out_shape=out,
        in_specs=[SMEM] * (1 + patches) + [VMEM] * (1 + patches),
        out_specs=VMEM,
        scratch_shapes=[pltpu.SMEM((blocks + 1,), jnp.int32)],
        compiler_params=params,
        name="base",
    )(info, *dests, positions, packed, *arrived)
    outs = pl.pallas_call(
        functools.partial(finish_kernel, subs, slots),
        out_shape=(out, out),
        in_specs=[SMEM] * (1 + subs) + [VMEM] * (1 + subs),
        out_specs=(VMEM, VMEM),
        compiler_params=params,
        name="finish",
    )(info, *lists, *shares, base)
    return tuple(jnp.transpose(a, (1, 0, 2)) for a in outs)


def solution(mesh):
    by_list = P(("grp", "patch", "sub"))
    halves = P(("grp", "patch", "sub"), None, "pair")
    whole = P(("grp", "patch"), None, None)
    return jax.shard_map(
        local,
        mesh=mesh,
        in_specs=(whole, whole, halves, by_list, by_list, by_list, by_list),
        out_specs=(halves, halves),
        check_vma=False,
    )
```

```python
import functools
import math

import jax
import jax.numpy as jnp
from jax import lax
from jax.experimental import pallas as pl
from jax.experimental.pallas import tpu as pltpu
from jax.sharding import PartitionSpec as P

PTS = 96
EPSILON_SQ = 0.0625
SCALE_8PI = 1.0 / (8.0 * math.pi)
STIFFNESS = 0.25
CHUNK = 768
GROUP = 4

VMEM = pl.BlockSpec(memory_space=pltpu.VMEM)
SMEM = pl.BlockSpec(memory_space=pltpu.SMEM)


def cilium_forces(points, drive):
    width = points.shape[1]
    place = lax.broadcasted_iota(jnp.int32, points.shape, 1) % PTS
    before = jnp.where(place == 0, points, pltpu.roll(points, 1, 1))
    after = jnp.where(place == PTS - 1, points, pltpu.roll(points, width - 1, 1))
    return STIFFNESS * (before + after - 2.0 * points) + drive


def half_at(side, half):
    return pl.ds(pl.multiple_of(side * half, 128), half)


def rows_at(ref, index, lanes=slice(None), first=0):
    return jnp.concatenate(
        [ref[c, pl.ds(index, 1), lanes] for c in range(first, first + 3)], axis=0
    )


def pack_history_kernel(panels, info_ref, dest_ref, hist_ref, out_ref, taken):
    patches = out_ref.shape[0]
    me = info_ref[0]
    for o in range(patches):
        taken[o] = 0

    def one(b, carry):
        owner = dest_ref[b] // panels
        rel = lax.rem(owner - me + patches, patches)
        row = taken[rel]
        taken[rel] = row + 1
        for c in range(3):
            out_ref[rel, c, pl.ds(row, 1), :] = hist_ref[c, pl.ds(b, 1), :]
        return carry

    lax.fori_loop(0, hist_ref.shape[1], one, 0, unroll=4)


def pack_near_kernel(slots, info_ref, left_ref, right_ref, pos_ref, drive_ref, to_left, to_right):
    panels = pos_ref.shape[1]
    half = to_left.shape[2]
    lanes = half_at(info_ref[2], half)

    def one(i, msg_ref, out_ref, first):
        wanted = msg_ref[i] - first

        @pl.when((wanted >= 0) & (wanted < panels) & (i < msg_ref[slots]))
        def _():
            points = rows_at(pos_ref, wanted, lanes)
            forces = cilium_forces(points, rows_at(drive_ref, wanted, lanes))
            for c in range(3):
                out_ref[c, pl.ds(i, 1), :] = points[c : c + 1]
                out_ref[3 + c, pl.ds(i, 1), :] = forces[c : c + 1]

    def both(i, carry):
        one(i, right_ref, to_right, 0)
        one(i, left_ref, to_left, 2 * panels)
        return carry

    lax.fori_loop(0, slots, both, 0)


def split3(value):
    high = value.astype(jnp.bfloat16).astype(jnp.float32)
    rest = value - high
    middle = rest.astype(jnp.bfloat16).astype(jnp.float32)
    return high, middle, rest - middle


def tile_velocity(target, sources):
    center = jnp.mean(target, axis=1, keepdims=True)
    x = target - center
    width = x.shape[1]
    xx = jnp.sum(x * x, axis=0, keepdims=True)
    ones = jnp.ones((1, width), jnp.float32)
    none = jnp.zeros((3, width), jnp.float32)
    qh, qm, ql = split3(jnp.concatenate([-2.0 * x, ones, xx + EPSILON_SQ, none], axis=0))
    right = jnp.concatenate([qh, qm, qh, qm, ql, qh], axis=0).astype(jnp.bfloat16)
    total = small = None
    for points, force in sources:
        y = points - center
        length = y.shape[1]
        yy = jnp.sum(y * y, axis=0, keepdims=True)
        yf = jnp.sum(y * force, axis=0, keepdims=True)
        ones = jnp.ones((1, length), jnp.float32)
        none = jnp.zeros((3, length), jnp.float32)
        ph, pm, pw = split3(jnp.concatenate([y, yy, ones, none], axis=0))
        left = jnp.concatenate([ph, ph, pm, pm, ph, pw], axis=0).astype(jnp.bfloat16)
        pad = jnp.zeros((5, length), jnp.float32)
        weights = jnp.concatenate(
            [force, yf, force * y[0:1], yf * y[0:1], force * y[1:2], yf * y[1:2],
             force * y[2:3], yf * y[2:3], force * yy, pad],
            axis=0,
        )
        weights = jnp.concatenate(split3(weights), axis=0).astype(jnp.bfloat16)
        tail_rows = 2 * weights.shape[0] // 3
        for start in range(0, length, CHUNK):
            stop = min(start + CHUNK, length)
            squared = lax.dot_general(
                left[:, start:stop], right, (((0,), (0,)), ((), ())),
                preferred_element_type=jnp.float32,
            )
            inverse = lax.rsqrt(squared)
            cube = inverse * inverse * inverse
            high = cube.astype(jnp.bfloat16)
            low = (cube - high.astype(jnp.float32)).astype(jnp.bfloat16)
            some = weights[:, start:stop]
            part = jnp.dot(some, high, preferred_element_type=jnp.float32)
            tail = jnp.dot(some[:tail_rows], low, preferred_element_type=jnp.float32)
            total = part if total is None else total + part
            small = tail if small is None else small + tail
    rows = total.shape[0] // 3
    total = total[2 * rows :] + small[rows:] + total[rows : 2 * rows] + small[:rows] + total[:rows]
    plain, along = total[0:3], total[3:4]
    by_y = [total[4 + 4 * c : 7 + 4 * c] for c in range(3)]
    along_y = [total[7 + 4 * c : 8 + 4 * c] for c in range(3)]
    lengths = total[16:19]
    direct = (xx + 2.0 * EPSILON_SQ) * plain + lengths
    for c in range(3):
        direct = direct - 2.0 * x[c : c + 1] * by_y[c]
    shared = jnp.sum(x * plain, axis=0, keepdims=True) - along
    outs = []
    for c in range(3):
        outs.append(
            SCALE_8PI
            * (
                direct[c : c + 1]
                + x[c : c + 1] * shared
                - jnp.sum(x * by_y[c], axis=0, keepdims=True)
                + along_y[c]
            )
        )
    return outs


def each_slot(chosen, count, wanted, work):
    def note(i, found):
        chosen[found] = i
        return found + wanted(i).astype(jnp.int32)

    found = lax.fori_loop(0, count, note, 0)

    def group(j, carry):
        for k in range(GROUP):
            work(chosen[jnp.minimum(j * GROUP + k, found - 1)])
        return carry

    lax.fori_loop(0, (found + GROUP - 1) // GROUP, group, 0)


def own_tiles_kernel(info_ref, source_ref, target_ref, count_ref, pos_ref, drive_ref, out_ref, chosen):
    panels = pos_ref.shape[1]
    half = out_ref.shape[2]
    lanes = half_at(info_ref[2], half)

    def wanted(i):
        return source_ref[i] // panels == 1

    def work(i):
        source = source_ref[i] - panels
        points = rows_at(pos_ref, source)
        forces = cilium_forces(points, rows_at(drive_ref, source))
        rows = tile_velocity(rows_at(pos_ref, target_ref[i], lanes), [(points, forces)])
        for c in range(3):
            out_ref[c, pl.ds(i, 1), :] = rows[c]

    each_slot(chosen, count_ref[0], wanted, work)


def near_tiles_kernel(
    info_ref, source_ref, target_ref, count_ref, pos_ref, lefta, leftb, righta, rightb, own_ref,
    out_ref, chosen
):
    panels = pos_ref.shape[1]
    half = out_ref.shape[2]
    lanes = half_at(info_ref[2], half)
    out_ref[...] = own_ref[...]

    def wanted(i):
        return source_ref[i] // panels != 1

    def work(i):
        is_left = source_ref[i] < panels

        def both(first):
            return jnp.concatenate(
                [
                    jnp.where(is_left, rows_at(a, i, first=first), rows_at(b, i, first=first))
                    for a, b in ((lefta, righta), (leftb, rightb))
                ],
                axis=1,
            )

        rows = tile_velocity(rows_at(pos_ref, target_ref[i], lanes), [(both(0), both(3))])
        for c in range(3):
            out_ref[c, pl.ds(i, 1), :] = rows[c]

    each_slot(chosen, count_ref[0], wanted, work)


def base_kernel(patches, *refs):
    info_ref = refs[0]
    dests = refs[1 : 1 + patches]
    pos_ref, packed_ref = refs[1 + patches : 3 + patches]
    arrived = refs[3 + patches : 2 + 2 * patches]
    out_ref, places = refs[-2:]
    blocks, half = out_ref.shape[1:]
    panels = pos_ref.shape[1]
    me, side = info_ref[0], info_ref[2]
    first = pl.multiple_of(info_ref[1] * blocks, blocks)
    for shift in range(patches):
        old_ref = packed_ref.at[0] if shift == 0 else arrived[shift - 1]

        def note(b, found, shift=shift):
            places[found] = b
            return found + (dests[shift][b] // panels == me).astype(jnp.int32)

        lax.fori_loop(0, blocks, note, 0, unroll=8)

        def put(r, carry, old_ref=old_ref):
            for c in range(3):
                out_ref[c, pl.ds(places[r], 1), :] = old_ref[c, pl.ds(r, 1), :]
            return carry

        lax.fori_loop(0, old_ref.shape[1], put, 0, unroll=True)
    mine = pos_ref[:, pl.ds(first, blocks), half_at(side, half)]
    out_ref[...] = (4.0 * mine - out_ref[...]) / 3.0


def finish_kernel(subs, slots, *refs):
    info_ref = refs[0]
    lists = refs[1 : 1 + subs]
    shares = refs[1 + subs : 1 + 2 * subs]
    base_ref, vel_ref, new_ref = refs[1 + 2 * subs :]
    blocks = vel_ref.shape[1]
    first = info_ref[1] * blocks
    vel_ref[...] = jnp.zeros_like(vel_ref)
    for list_ref, share_ref in zip(lists, shares):

        def add(i, carry, list_ref=list_ref, share_ref=share_ref):
            place = list_ref[i] - first

            @pl.when((place >= 0) & (place < blocks))
            def _():
                for c in range(3):
                    vel_ref[c, pl.ds(place, 1), :] += share_ref[c, pl.ds(i, 1), :]

            return carry

        lax.fori_loop(0, list_ref[slots], add, 0)
    new_ref[...] = base_ref[...] + (1.0 / 3.0) * vel_ref[...]


def local(positions, drive, history, hist_dest, tile_target, tile_source, tile_count):
    panels = positions.shape[0]
    panel_len = positions.shape[2]
    patches, subs, pairs = (lax.axis_size(a) for a in ("patch", "sub", "pair"))
    half = panel_len // pairs
    slots = tile_target.shape[0]
    blocks = history.shape[0]
    per_peer = (blocks + patches - 1) // patches
    info = jnp.stack(
        [lax.axis_index("patch"), lax.axis_index("sub"), lax.axis_index("pair")]
    ).astype(jnp.int32)
    f32 = jnp.float32
    params = pltpu.CompilerParams(vmem_limit_bytes=48 * 1024 * 1024)
    positions, drive, history = (jnp.transpose(a, (1, 0, 2)) for a in (positions, drive, history))

    def shifted(value, axis, shift):
        count = lax.axis_size(axis)
        return lax.ppermute(value, axis, [(i, (i + shift) % count) for i in range(count)])

    message = jnp.concatenate([tile_source, tile_count, hist_dest])
    heard = [message] + [shifted(message, "patch", s) for s in range(1, patches)]
    targets = jnp.concatenate([tile_target, tile_count])
    lists = [targets] + [shifted(targets, "sub", s) for s in range(1, subs)]

    packed = pl.pallas_call(
        functools.partial(pack_history_kernel, panels),
        out_shape=jax.ShapeDtypeStruct((patches, 3, per_peer, half), f32),
        in_specs=[SMEM, SMEM, VMEM],
        out_specs=VMEM,
        scratch_shapes=[pltpu.SMEM((patches,), jnp.int32)],
        compiler_params=params,
        name="pack_history",
    )(info, hist_dest, history)
    packed, *heard = lax.optimization_barrier((packed, *heard))
    dests = [hist_dest] + [m[slots + 1 :] for m in heard[1:]]

    near = jax.ShapeDtypeStruct((6, slots, half), f32)
    to_left, to_right = pl.pallas_call(
        functools.partial(pack_near_kernel, slots),
        out_shape=(near, near),
        in_specs=[SMEM, SMEM, SMEM, VMEM, VMEM],
        out_specs=(VMEM, VMEM),
        compiler_params=params,
        name="pack_near",
    )(info, heard[1], heard[-1], positions, drive)

    up = [(i, i + 1) for i in range(patches - 1)]
    from_left = lax.ppermute(to_right, "patch", up)
    from_right = lax.ppermute(to_left, "patch", [(b, a) for a, b in up])

    arrived = [shifted(packed[s], "patch", s) for s in range(1, patches)]

    tiles = jax.ShapeDtypeStruct((3, slots, half), f32)
    chosen = [pltpu.SMEM((slots + 1,), jnp.int32)]
    pairs_all = slots * half * panel_len
    cost = pl.CostEstimate(
        flops=pairs_all * 256, bytes_accessed=4 * positions.size * 2, transcendentals=pairs_all
    )
    own = pl.pallas_call(
        own_tiles_kernel,
        out_shape=tiles,
        in_specs=[SMEM] * 4 + [VMEM] * 2,
        out_specs=VMEM,
        scratch_shapes=chosen,
        compiler_params=params,
        cost_estimate=cost,
        name="own_tiles",
    )(info, tile_source, tile_target, tile_count, positions, drive)

    other_left = shifted(from_left, "pair", 1)
    other_right = shifted(from_right, "pair", 1)
    share = pl.pallas_call(
        near_tiles_kernel,
        out_shape=tiles,
        in_specs=[SMEM] * 4 + [VMEM] * 6,
        out_specs=VMEM,
        scratch_shapes=chosen,
        compiler_params=params,
        cost_estimate=cost,
        name="near_tiles",
    )(info, tile_source, tile_target, tile_count, positions,
      from_left, other_left, from_right, other_right, own)
    shares = [share] + [shifted(share, "sub", s) for s in range(1, subs)]
    _, *arrived = lax.optimization_barrier((share, *arrived))

    out = jax.ShapeDtypeStruct((3, blocks, half), f32)
    base = pl.pallas_call(
        functools.partial(base_kernel, patches),
        out_shape=out,
        in_specs=[SMEM] * (1 + patches) + [VMEM] * (1 + patches),
        out_specs=VMEM,
        scratch_shapes=[pltpu.SMEM((blocks + 1,), jnp.int32)],
        compiler_params=params,
        name="base",
    )(info, *dests, positions, packed, *arrived)
    outs = pl.pallas_call(
        functools.partial(finish_kernel, subs, slots),
        out_shape=(out, out),
        in_specs=[SMEM] * (1 + subs) + [VMEM] * (1 + subs),
        out_specs=(VMEM, VMEM),
        compiler_params=params,
        name="finish",
    )(info, *lists, *shares, base)
    return tuple(jnp.transpose(a, (1, 0, 2)) for a in outs)


def solution(mesh):
    by_list = P(("grp", "patch", "sub"))
    halves = P(("grp", "patch", "sub"), None, "pair")
    whole = P(("grp", "patch"), None, None)
    return jax.shard_map(
        local,
        mesh=mesh,
        in_specs=(whole, whole, halves, by_list, by_list, by_list, by_list),
        out_specs=(halves, halves),
        check_vma=False,
    )
```
